32 devices in a mesh: section: 4 (over y, x), expert: 8 (over z, core).
Axes of the slice: x: 2, y: 2, z: 4, core: 2. Of those that a mesh axis runs over, the one named last changes fastest.
Arguments:
- tokens: bfloat16 [4, 2, 512, 2048], P('section', None, 'expert'), may hold values from -6 to 6
- routes: int32 [4, 1, 2, 512, 2], P('section', None, None, 'expert'), may hold values from 0 to 7, all different within a row; in each aligned block of 64 rows (0 to 63, 64 to 127, ..., all dimensions but the last counted through in order) at most 20 rows name the same one
- norm_gain: bfloat16 [4, 2048], P('section'), may hold values from 0.5 to 1.5
- router: bfloat16 [4, 2048, 8], P('section')
- gate_weight: bfloat16 [4, 2048, 8192], P('section', None, 'expert'), may hold values from -0.125 to 0.125
- up_weight: bfloat16 [4, 2048, 8192], P('section', None, 'expert'), may hold values from -0.125 to 0.125
- down_weight: bfloat16 [4, 8192, 2048], P('section', 'expert'), may hold values from -0.1875 to 0.1875
Outputs:
- mixed: bfloat16 [4, 2, 512, 2048], P('section', None, 'expert')
The draws below stay inside these ranges and needn't reach their ends.
Inputs may be any that keep to these rules, and one draw needn't show every extreme that they name: `routes`: each token names 2 different experts. Within the 64 rows of one device for one start section, layer step and micro-batch, no expert is named more than 20 times, a bound that some block reaches.
All inputs are finite; a program needn't handle non-finite values.
Results may differ from the reference program's by a relative error of at most 0.0045.
Values may be sent and summed in bfloat16 or wider, within the bound.
No kernel may reach another device: no remote copies, remote signals or barrier semaphores. Data moves between devices by JAX's collectives and lax.ppermute only.
A program may use at most 128 MiB of HBM per device.

```python
import math
import jax
import jax.numpy as jnp
import numpy as np
from jax import lax

D = 2048
FF = 1024
EXPERTS = 8
TOP = 2
MICRO = 2
ROUNDS = 1
TOK_DEV = 64
CAP = 20
LAYERS = 4
HOMES = 4
TOKENS = 512
N_EXPERT = 8


def draw_router(key, part):
    key = jax.random.fold_in(key, 11)
    spread = 0.5 * (1.0 / D) ** 0.5
    values = jax.random.normal(key, (LAYERS, D, EXPERTS), jnp.float32) * spread
    return values.astype(jnp.bfloat16)


def block_scale(own_key, dims, pieces, smallest, high):
    loudness = 1.0
    for axis_at, blocks in pieces:
        steps = jax.random.uniform(jax.random.fold_in(jax.random.fold_in(own_key, 6), axis_at), (blocks,), jnp.float32, smallest / len(pieces), high / len(pieces))
        loudness = loudness * jnp.repeat(jnp.exp(steps), dims[axis_at] // blocks).reshape((-1,) + (1,) * (len(dims) - 1 - axis_at))
    return loudness


def assign_block(key, own, number, rows, amount, top, limit, slope):
    sequence = jax.random.permutation(key, amount)
    crowded, usual = shares(amount, rows * top, limit, slope, True), shares(amount, rows * top, limit, slope, False)
    places = jnp.arange(amount)

    def named(lengths, turn):
        used = int((lengths > 0).sum())
        fixed = max(1, used // 4)
        moved = fixed + (places - fixed + turn * (used - fixed)) % max(1, amount - fixed)
        return jnp.zeros((amount,), jnp.int32).at[sequence[jnp.where(places < fixed, places, moved)]].set(jnp.asarray(lengths, jnp.int32))

    lengths = jnp.where(number % 4 == 0, named(crowded, number // 4), named(usual, number - number // 4 - 1))
    mixed = jax.random.permutation(jax.random.fold_in(own, 3), amount)
    donor, receiver = mixed[0:amount // 2 * 2:2], mixed[1:amount // 2 * 2:2]
    room = jnp.minimum(lengths[donor] - 1, limit - lengths[receiver]) // 2
    room = jnp.where((donor == sequence[0]) | (receiver == sequence[0]) | (lengths[receiver] == 0), 0, jnp.maximum(room, 0))
    moved = jax.random.randint(jax.random.fold_in(own, 4), (amount // 2,), 0, 1 << 20) % (room + 1)
    lengths = lengths.at[donor].add(-moved).at[receiver].add(moved)
    items = jnp.searchsorted(jnp.cumsum(lengths), jnp.arange(rows * top), side="right").astype(jnp.int32)
    listing = items.reshape(top, rows).T
    listing = listing[jax.random.permutation(jax.random.fold_in(own, 1), rows)]
    turn = jax.random.randint(jax.random.fold_in(own, 2), (rows, 1), 0, top)
    return jnp.take_along_axis(listing, (jnp.arange(top)[None, :] + turn) % top, axis=1)


def shares(number_of, total, limit, lean, full):
    portions = [(1 << 20) // math.isqrt(grade ** lean) + 1 for grade in range(1, number_of + 1)]
    largest = limit if full else min(limit, max(-(-total // number_of), total * portions[0] // sum(portions)))
    least = 1 if total - largest >= number_of - 1 else 0
    counts, spare = [largest] + [least] * (number_of - 1), total - largest - least * (number_of - 1)
    while spare > 0:
        candidates = [i for i in range(1, number_of) if counts[i] < largest] or [i for i in range(1, number_of) if counts[i] < limit]
        pool, remaining = sum([portions[i] for i in candidates]), spare
        for i in candidates:
            more = min(limit - counts[i], max(1, remaining * portions[i] // pool), spare)
            counts[i] = counts[i] + more
            spare = spare - more
    return np.array(counts)


def centred(own_key, extent, scale, limit, pieces=(), kind=jnp.bfloat16):
    values = jax.random.normal(own_key, extent, jnp.float32) * scale
    if len(pieces) > 0:
        values = block_scale(own_key, extent, pieces, -0.22, 0.18) * values
    return jnp.clip(values, min=-limit, max=limit).astype(kind)


def setup_inputs(seed: int = 0) -> dict:
    keys = jax.random.split(jax.random.key(seed), 8)
    tokens = centred(keys[0], (HOMES, MICRO, TOKENS, D), 1.0, 6.0, ((0, 4), (2, 8)))
    routes_keys = jax.random.split(jax.random.fold_in(keys[1], 1), HOMES * ROUNDS * MICRO * TOKENS // TOK_DEV)
    routes_turns = jax.random.permutation(jax.random.fold_in(keys[1], 3), HOMES * ROUNDS * MICRO * TOKENS // TOK_DEV)
    routes = jax.vmap(lambda own, number: assign_block(jax.random.fold_in(keys[1], 2), own, number, TOK_DEV, EXPERTS, TOP, CAP, 2))(routes_keys, routes_turns).reshape((HOMES, ROUNDS, MICRO, TOKENS, TOP))
    norm_gain = jnp.clip(1.0 + 0.1 * jax.random.normal(keys[2], (LAYERS, D), jnp.float32), 0.5, 1.5).astype(jnp.bfloat16)
    router = draw_router(jax.random.fold_in(keys[7], 71), 0)
    gate_weight = centred(keys[4], (LAYERS, D, EXPERTS * FF), D ** -0.5, 0.125, ((0, 4), (2, 8)))
    up_weight = centred(keys[5], (LAYERS, D, EXPERTS * FF), D ** -0.5, 0.125, ((0, 4), (2, 8)))
    down_weight = centred(keys[6], (LAYERS, EXPERTS * FF, D), FF ** -0.5, 0.1875, ((0, 4), (1, 8)))
    return {"tokens": tokens, "routes": routes, "norm_gain": norm_gain, "router": router, "gate_weight": gate_weight, "up_weight": up_weight, "down_weight": down_weight}


epsilon = 1e-06

def moe_layer(current, routing, norm_gain, router, gate_weight, up_weight, down_weight):
    experts = router.shape[1]
    features = current.shape[1]
    chosen_count = routing.shape[1]
    groups = N_EXPERT // experts
    hidden_units = gate_weight.shape[1] // experts
    slice_units = hidden_units // groups
    capacity = N_EXPERT * CAP
    wide_rows = current.astype(jnp.float32)
    normed = (wide_rows * lax.rsqrt(lax.optimization_barrier(jnp.mean(wide_rows * wide_rows, axis=-1, keepdims=True)) + epsilon) * norm_gain.astype(jnp.float32)).astype(jnp.bfloat16)
    logits = jnp.dot(normed, router, preferred_element_type=jnp.float32)
    chosen = jnp.take_along_axis(logits, routing, axis=1)
    route_weight = jax.nn.softmax(chosen, axis=-1)
    matches = jnp.any(routing[:, :, None] == jnp.arange(experts, dtype=jnp.int32)[None, None, :], axis=1)
    running = jnp.cumsum(matches.astype(jnp.int32), axis=0) - 1
    slot_index = jnp.take_along_axis(running, routing, axis=1).astype(jnp.int32)
    packed = jnp.zeros((experts, capacity, features), jnp.bfloat16).at[routing.reshape(-1), slot_index.reshape(-1)].set(jnp.repeat(normed, chosen_count, axis=0))
    gate_cube = gate_weight.astype(jnp.float32).reshape(features, experts, hidden_units)
    up_cube = up_weight.astype(jnp.float32).reshape(features, experts, hidden_units)
    packed_wide = packed.astype(jnp.float32)
    gate_act = jnp.einsum('erd,def->erf', packed_wide, gate_cube)
    up_act = jnp.einsum('erd,def->erf', packed_wide, up_cube)
    hidden = (jax.nn.silu(gate_act) * up_act).astype(jnp.bfloat16)
    hidden_four = hidden.astype(jnp.float32).reshape(experts, capacity, groups, slice_units)
    down_four = down_weight.astype(jnp.float32).reshape(experts, groups, slice_units, features)
    partial_value = jnp.einsum('ergh,eghd->ergd', hidden_four, down_four).astype(jnp.bfloat16)
    summed = lax.optimization_barrier(jnp.sum(partial_value.astype(jnp.float32), axis=2))
    picked = summed[routing, slot_index]
    added = lax.optimization_barrier(jnp.sum(route_weight[:, :, None] * picked, axis=1))
    return (wide_rows + added).astype(jnp.bfloat16)

def reference(tokens, routes, norm_gain, router, gate_weight, up_weight, down_weight):

    def one_home(home_index):
        current = tokens[home_index]
        for layer_step in range(ROUNDS):
            layer_index = (home_index + 1 + layer_step) % LAYERS
            results = []
            for batch_index in range(MICRO):
                results.append(moe_layer(current[batch_index], routes[home_index, layer_step, batch_index], norm_gain[layer_index], router[layer_index], gate_weight[layer_index], up_weight[layer_index], down_weight[layer_index]))
            current = jnp.stack(results)
        return current
    return lax.map(one_home, jnp.arange(HOMES, dtype=jnp.int32))
```

```python
import functools

import jax
import jax.numpy as jnp
from jax import lax
from jax.experimental import pallas as pl
from jax.experimental.pallas import tpu as pltpu
from jax.sharding import PartitionSpec as P

CAP = 20
FIRST = 16
epsilon = 1e-06
HOME = ("section", "expert")


def moved(block, by, flip):
    sections, width = lax.axis_size("section"), lax.axis_size("expert")
    pairs = [
        (s * width + e, (s + by) % sections * width + (e ^ flip))
        for s in range(sections)
        for e in range(width)
    ]
    return lax.ppermute(block, HOME, pairs)


def ranks(me, chosen, width, groups):
    tokens = chosen.shape[1]
    owner = lax.broadcasted_iota(jnp.int32, (width, tokens), 0) ^ me
    expert = owner // groups if groups > 1 else owner
    first = chosen[0:1, :] == expert
    match = first | (chosen[1:2, :] == expert)
    before = lax.broadcasted_iota(jnp.int32, (tokens, tokens), 0) < lax.broadcasted_iota(
        jnp.int32, (tokens, tokens), 1
    )
    rank = jnp.dot(
        match.astype(jnp.bfloat16), before.astype(jnp.bfloat16), preferred_element_type=jnp.float32
    ).astype(jnp.int32)
    return first, jnp.where(match, rank, -1)


def slots_of(rank, start, size):
    width, tokens = rank.shape
    place = lax.broadcasted_iota(jnp.int32, (width, size, tokens), 1) + start
    return rank[:, None, :] == place


def pack_kernel(width, groups, parts, me_ref, chosen_ref, rows_ref, *out_refs):
    _, rank = ranks(me_ref[0], chosen_ref[...], width, groups)
    rows = rows_ref[...]
    half = width // 2
    for part, (start, size) in enumerate(parts):
        select = slots_of(rank, start, size).astype(jnp.float32)
        select = select.reshape(width * size, rows.shape[0]).astype(jnp.bfloat16)
        for j in range(half):
            block = select[2 * j * size : 2 * (j + 1) * size]
            out_refs[part * half + j][...] = jnp.dot(
                block, rows, preferred_element_type=jnp.float32
            ).astype(jnp.bfloat16)


def weight_kernel(width, groups, parts, me_ref, chosen_ref, rows_ref, gain_ref, router_ref, *out_refs):
    chosen = chosen_ref[...]
    first, rank = ranks(me_ref[0], chosen, width, groups)
    normed = normalised(rows_ref[...], gain_ref[...])
    logits = lax.dot_general(
        router_ref[...], normed, (((1,), (1,)), ((), ())), preferred_element_type=jnp.float32
    )
    names = lax.broadcasted_iota(jnp.int32, logits.shape, 0)
    one = jnp.sum(jnp.where(names == chosen[0:1, :], logits, 0.0), axis=0, keepdims=True)
    two = jnp.sum(jnp.where(names == chosen[1:2, :], logits, 0.0), axis=0, keepdims=True)
    top = jnp.maximum(one, two)
    one, two = jnp.exp(one - top), jnp.exp(two - top)
    total = one + two
    weight = jnp.where(first, one / total, two / total)
    for part, (start, size) in enumerate(parts):
        wide = jnp.where(slots_of(rank, start, size), weight[:, None, :], 0.0)
        wide = wide.reshape(width * size, weight.shape[1])
        high = wide.astype(jnp.bfloat16)
        out_refs[part][0] = high
        out_refs[part][1] = (wide - high.astype(jnp.float32)).astype(jnp.bfloat16)


def normalised(rows, gain):
    wide = rows.astype(jnp.float32)
    scale = lax.rsqrt(jnp.mean(wide * wide, axis=-1, keepdims=True) + epsilon)
    return (wide * scale * gain.astype(jnp.float32)).astype(jnp.bfloat16)


def expert_kernel(half, size, steps, *refs):
    blocks, (passed_ref, gain_ref, gate_ref, up_ref, down_ref) = refs[:half], refs[half : half + 5]
    keep_ref, give_ref, normed_ref, total_ref = refs[half + 5 :]
    step = pl.program_id(0)

    @pl.when(step == 0)
    def _():
        gain = gain_ref[...]
        for j in range(half):
            normed_ref[j * size : (j + 1) * size] = normalised(blocks[j][0:size], gain)
        normed_ref[half * size :] = normalised(passed_ref[...], gain)

    normed = normed_ref[...]
    gate = jnp.dot(normed, gate_ref[...], preferred_element_type=jnp.float32)
    up = jnp.dot(normed, up_ref[...], preferred_element_type=jnp.float32)
    hidden = (gate / (1.0 + jnp.exp(-gate)) * up).astype(jnp.bfloat16)
    share = jnp.dot(hidden, down_ref[...], preferred_element_type=jnp.float32)

    @pl.when(step == 0)
    def _():
        total_ref[...] = share

    @pl.when(step > 0)
    def _():
        total_ref[...] += share

    @pl.when(step == steps - 1)
    def _():
        keep_ref[...] = total_ref[0 : half * size].astype(jnp.bfloat16)
        give_ref[...] = total_ref[half * size :].astype(jnp.bfloat16)


def combine_kernel(sizes, half, rows_ref, *refs):
    weights, blocks, out_ref = refs[: len(sizes)], refs[len(sizes) : -1], refs[-1]
    total = rows_ref[...].astype(jnp.float32)
    for part, size in enumerate(sizes):
        values = jnp.concatenate([ref[...] for ref in blocks[part * half : (part + 1) * half]], axis=0)
        for term in range(2):
            total += jnp.dot(weights[part][term], values, preferred_element_type=jnp.float32)
    out_ref[...] = total.astype(jnp.bfloat16)


SMEM = pl.BlockSpec(memory_space=pltpu.SMEM)
VMEM = pl.BlockSpec(memory_space=pltpu.VMEM)
LIMIT = 40 * 1024 * 1024


def run_experts(blocks, passed, size, gain, gate, up, down):
    half, features = len(blocks), gain.shape[1]
    rows, units = 2 * half * size, gate.shape[1]
    tile = min(256, units)
    steps = units // tile
    fixed = lambda shape: pl.BlockSpec(shape, lambda i: (0, 0))
    part = jax.ShapeDtypeStruct((half * size, features), jnp.bfloat16)
    return pl.pallas_call(
        functools.partial(expert_kernel, half, size, steps),
        grid=(steps,),
        in_specs=[fixed((2 * size, features))] * half
        + [
            fixed((half * size, features)),
            fixed((1, features)),
            pl.BlockSpec((features, tile), lambda i: (0, i)),
            pl.BlockSpec((features, tile), lambda i: (0, i)),
            pl.BlockSpec((tile, features), lambda i: (i, 0)),
        ],
        out_specs=[fixed((half * size, features))] * 2,
        out_shape=[part, part],
        scratch_shapes=[
            pltpu.VMEM((rows, features), jnp.bfloat16),
            pltpu.VMEM((rows, features), jnp.float32),
        ],
        compiler_params=pltpu.CompilerParams(vmem_limit_bytes=LIMIT),
        cost_estimate=pl.CostEstimate(
            flops=6 * rows * features * units,
            bytes_accessed=6 * features * units + 8 * rows * features,
            transcendentals=rows * units,
        ),
        name="experts",
    )(*blocks, passed, gain, gate, up, down)


def shards(tokens, routes, norm_gain, router, gate_weight, up_weight, down_weight):
    batches, count, features = tokens.shape[1:]
    experts = router.shape[2]
    width = lax.axis_size("expert")
    groups, half = width // experts, width // 2
    parts = ((0, FIRST), (FIRST, batches * CAP - FIRST))
    rows = tokens.reshape(batches * count, features)
    chosen = routes.reshape(batches * count, 2).T
    me = lax.axis_index("expert").astype(jnp.int32).reshape(1)

    outgoing = pl.pallas_call(
        functools.partial(pack_kernel, width, groups, parts),
        in_specs=[SMEM, VMEM, VMEM],
        out_specs=[VMEM] * (2 * half),
        out_shape=[
            jax.ShapeDtypeStruct((2 * size, features), jnp.bfloat16)
            for _, size in parts
            for _ in range(half)
        ],
        compiler_params=pltpu.CompilerParams(vmem_limit_bytes=LIMIT),
        name="pack",
    )(me, chosen, rows)

    far_first = range(half - 1, -1, -1)
    returned = []
    arrived = []
    for part in range(len(parts)):
        got = {j: moved(outgoing[part * half + j], 1, 2 * j) for j in far_first}
        arrived.append([got[j] for j in range(half)])

    gain_there = moved(norm_gain, -1, 0)
    router_there = moved(router[0].T, -1, 0)
    weights = pl.pallas_call(
        functools.partial(weight_kernel, width, groups, parts),
        in_specs=[SMEM, VMEM, VMEM, VMEM, VMEM],
        out_specs=[VMEM] * 2,
        out_shape=[
            jax.ShapeDtypeStruct((2, width * size, batches * count), jnp.bfloat16)
            for _, size in parts
        ],
        compiler_params=pltpu.CompilerParams(vmem_limit_bytes=LIMIT),
        name="weights",
    )(me, chosen, rows, gain_there, router_there)
    weights = [jnp.swapaxes(weight, 1, 2) for weight in weights]

    for part, (_, size) in enumerate(parts):
        blocks = arrived[part]
        passed = moved(jnp.concatenate([block[size:] for block in blocks], axis=0), 0, 1)
        keep, give = run_experts(
            blocks, passed, size, norm_gain, gate_weight[0], up_weight[0], down_weight[0]
        )
        taken = moved(give, 0, 1)
        both = [
            jnp.concatenate([keep[j * size : (j + 1) * size], taken[j * size : (j + 1) * size]], axis=0)
            for j in range(half)
        ]
        got = {j: moved(both[j], -1, 2 * j) for j in far_first}
        returned += [got[j] for j in range(half)]

    columns = min(512, features)
    mixed = pl.pallas_call(
        functools.partial(combine_kernel, [size for _, size in parts], half),
        grid=(features // columns,),
        in_specs=[pl.BlockSpec((batches * count, columns), lambda i: (0, i))]
        + [pl.BlockSpec(weight.shape, lambda i: (0, 0, 0)) for weight in weights]
        + [pl.BlockSpec((block.shape[0], columns), lambda i: (0, i)) for block in returned],
        out_specs=pl.BlockSpec((batches * count, columns), lambda i: (0, i)),
        out_shape=jax.ShapeDtypeStruct(rows.shape, jnp.bfloat16),
        compiler_params=pltpu.CompilerParams(vmem_limit_bytes=LIMIT),
        name="combine",
    )(rows, *weights, *returned)
    return mixed.reshape(tokens.shape)


def solution(mesh):
    placed = (
        P("section", None, "expert", None),
        P("section", None, None, "expert", None),
        P("section", None),
        P("section", None, None),
        P("section", None, "expert"),
        P("section", None, "expert"),
        P("section", "expert", None),
    )
    return jax.shard_map(
        shards,
        mesh=mesh,
        in_specs=placed,
        out_specs=P("section", None, "expert", None),
        check_vma=False,
    )
```

```python
import functools

import jax
import jax.numpy as jnp
from jax import lax
from jax.experimental import pallas as pl
from jax.experimental.pallas import tpu as pltpu
from jax.sharding import PartitionSpec as P

CAP = 20
epsilon = 1e-06
HOME = ("section", "expert")


def moved(block, by, flip):
    sections, width = lax.axis_size("section"), lax.axis_size("expert")
    pairs = [
        (s * width + e, (s + by) % sections * width + (e ^ flip))
        for s in range(sections)
        for e in range(width)
    ]
    return lax.ppermute(block, HOME, pairs)


def ranks(me, chosen, width, groups):
    tokens = chosen.shape[1]
    owner = lax.broadcasted_iota(jnp.int32, (width, tokens), 0) ^ me
    expert = owner // groups if groups > 1 else owner
    first = chosen[0:1, :] == expert
    match = first | (chosen[1:2, :] == expert)
    before = lax.broadcasted_iota(jnp.int32, (tokens, tokens), 0) < lax.broadcasted_iota(
        jnp.int32, (tokens, tokens), 1
    )
    rank = jnp.dot(
        match.astype(jnp.bfloat16), before.astype(jnp.bfloat16), preferred_element_type=jnp.float32
    ).astype(jnp.int32)
    return first, jnp.where(match, rank, -1)


def side_by_side(chosen_ref):
    return jnp.concatenate([chosen_ref[b] for b in range(chosen_ref.shape[0])], axis=1)


def pack_kernel(width, groups, flips, size, me_ref, *refs):
    chosen_refs, rows_refs, out_refs = refs[0:2], refs[2:4], refs[4:]
    for part in range(2):
        _, rank = ranks(me_ref[0], side_by_side(chosen_refs[part]), width, groups)
        rows = rows_refs[part][...]
        place = lax.broadcasted_iota(jnp.int32, (size, rank.shape[1]), 0)
        for out_ref, i in zip(out_refs, flips):
            select = (rank[i : i + 1] == place).astype(jnp.bfloat16)
            out_ref[part * size : (part + 1) * size] = jnp.dot(
                select, rows, preferred_element_type=jnp.float32
            ).astype(jnp.bfloat16)


def weight_kernel(
    width, groups, teams, size, me_ref, chosen_ref, rows_ref, there_ref, *out_refs
):
    chosen = side_by_side(chosen_ref)
    first, rank = ranks(me_ref[0], chosen, width, groups)
    experts = width // groups
    normed = normalised(rows_ref[...], there_ref[experts : experts + 1])
    logits = lax.dot_general(
        there_ref[0:experts], normed, (((1,), (1,)), ((), ())), preferred_element_type=jnp.float32
    )
    names = lax.broadcasted_iota(jnp.int32, logits.shape, 0)
    one = jnp.sum(jnp.where(names == chosen[0:1, :], logits, 0.0), axis=0, keepdims=True)
    two = jnp.sum(jnp.where(names == chosen[1:2, :], logits, 0.0), axis=0, keepdims=True)
    top = jnp.maximum(one, two)
    one, two = jnp.exp(one - top), jnp.exp(two - top)
    total = one + two
    weight = jnp.where(first, one / total, two / total)
    place = lax.broadcasted_iota(jnp.int32, (size, rank.shape[1]), 0)
    for part, team in enumerate(teams):
        for at, i in enumerate(team + tuple(i + 1 for i in team)):
            wide = jnp.where(rank[i : i + 1] == place, weight[i : i + 1], 0.0)
            high = wide.astype(jnp.bfloat16)
            span = slice(at * size, (at + 1) * size)
            out_refs[part][span] = high
            out_refs[2 + part][span] = (wide - high.astype(jnp.float32)).astype(jnp.bfloat16)


def normalised(rows, gain):
    wide = rows.astype(jnp.float32)
    scale = lax.rsqrt(jnp.mean(wide * wide, axis=-1, keepdims=True) + epsilon)
    return (wide * scale * gain.astype(jnp.float32)).astype(jnp.bfloat16)


def load_kernel(*refs):
    count = len(refs) // 2
    sources, held, sems = refs[:count], refs[count:-1], refs[-1]
    copies = [
        pltpu.make_async_copy(source, place, sems.at[k])
        for k, (source, place) in enumerate(zip(sources, held))
    ]
    for copy in copies:
        copy.start()
    for copy in copies:
        copy.wait()


def expert_kernel(count, size, *refs):
    blocks, (gain_ref, gate_ref, up_ref, down_ref) = refs[:count], refs[count : count + 4]
    outs, (normed_ref, hidden_ref) = refs[-2 - count : -2], refs[-2:]
    gain = gain_ref[...]
    for j in range(count):
        normed_ref[j * size : (j + 1) * size] = normalised(blocks[j][0:size], gain)
    normed = normed_ref[...]
    units, features = down_ref.shape
    step = min(256, units)
    for at in range(0, units, step):
        span = slice(at, at + step)
        gate = jnp.dot(normed, gate_ref[:, span], preferred_element_type=jnp.float32)
        up = jnp.dot(normed, up_ref[:, span], preferred_element_type=jnp.float32)
        hidden_ref[:, span] = (gate / (1.0 + jnp.exp(-gate)) * up).astype(jnp.bfloat16)
    hidden = hidden_ref[...]
    step = min(512, features)
    for at in range(0, features, step):
        span = slice(at, at + step)
        part = jnp.dot(hidden, down_ref[:, span], preferred_element_type=jnp.float32)
        part = part.astype(jnp.bfloat16)
        for j in range(count):
            outs[j][:, span] = part[j * size : (j + 1) * size]


def combine_kernel(base_ref, high_ref, low_ref, *refs):
    blocks, out_ref = refs[:-1], refs[-1]
    high, low = high_ref[...], low_ref[...]
    step = min(512, base_ref.shape[1])
    for at in range(0, base_ref.shape[1], step):
        span = slice(at, at + step)
        values = jnp.concatenate([ref[:, span] for ref in blocks], axis=0)
        total = base_ref[:, span].astype(jnp.float32)
        total += jnp.dot(high, values, preferred_element_type=jnp.float32)
        total += jnp.dot(low, values, preferred_element_type=jnp.float32)
        out_ref[:, span] = total.astype(out_ref.dtype)


def stack_kernel(count, start, size, *refs):
    out_ref = refs[-1]
    for k in range(count):
        out_ref[k * size : (k + 1) * size] = refs[k][start : start + size]


SMEM = pl.BlockSpec(memory_space=pltpu.SMEM)
VMEM = pl.BlockSpec(memory_space=pltpu.VMEM)
HBM = pl.BlockSpec(memory_space=pltpu.HBM)
ANY = pl.BlockSpec(memory_space=pl.ANY)
CHEAP = pl.CostEstimate(flops=1, bytes_accessed=1, transcendentals=0)
PARAMS = pltpu.CompilerParams(vmem_limit_bytes=20 * 1024 * 1024)


def load(*arrays):
    return pl.pallas_call(
        load_kernel,
        in_specs=[HBM] * len(arrays),
        out_specs=[VMEM] * len(arrays),
        out_shape=[pltpu.VMEM(array.shape, array.dtype) for array in arrays],
        scratch_shapes=[pltpu.SemaphoreType.DMA((len(arrays),))],
        compiler_params=pltpu.CompilerParams(vmem_limit_bytes=1024 * 1024),
        cost_estimate=CHEAP,
        name="load",
    )(*[pltpu.with_memory_space_constraint(array, pltpu.HBM) for array in arrays])


def stacked(blocks, start, size, after=()):
    return pl.pallas_call(
        functools.partial(stack_kernel, len(blocks), start, size),
        in_specs=[VMEM] * len(blocks) + [ANY] * len(after),
        out_specs=VMEM,
        out_shape=jax.ShapeDtypeStruct((len(blocks) * size, blocks[0].shape[1]), blocks[0].dtype),
        compiler_params=PARAMS,
        cost_estimate=CHEAP,
        name="stack",
    )(*blocks, *after)


def combine(base, high, low, blocks, dtype):
    return pl.pallas_call(
        combine_kernel,
        in_specs=[VMEM] * (3 + len(blocks)),
        out_specs=VMEM,
        out_shape=jax.ShapeDtypeStruct(base.shape, dtype),
        compiler_params=PARAMS,
        cost_estimate=CHEAP,
        name="combine",
    )(base, high.T, low.T, *blocks)


def run_experts(blocks, size, gain, gate, up, down, after=()):
    count, features = len(blocks), blocks[0].shape[1]
    rows, units = count * size, gate.shape[1]
    return pl.pallas_call(
        functools.partial(expert_kernel, count, size),
        in_specs=[VMEM] * (count + 4) + [ANY] * len(after),
        out_specs=[VMEM] * count,
        out_shape=[jax.ShapeDtypeStruct((size, features), jnp.bfloat16)] * count,
        scratch_shapes=[
            pltpu.VMEM((rows, features), jnp.bfloat16),
            pltpu.VMEM((rows, units), jnp.bfloat16),
        ],
        compiler_params=PARAMS,
        cost_estimate=CHEAP,
        name="experts",
    )(*blocks, gain, gate, up, down, *after)


def shards(tokens, routes, norm_gain, router, gate_weight, up_weight, down_weight):
    batches, count, features = tokens.shape[1:]
    experts = router.shape[2]
    width = lax.axis_size("expert")
    groups, size = width // experts, batches * CAP
    flips = tuple(range(width - 2, -1, -2))
    teams = [flips[len(flips) // 2 :], flips[: len(flips) // 2]]
    flips = teams[0] + teams[1]
    rows = tokens.reshape(batches * count, features)
    chosen = jnp.swapaxes(routes[0, 0], 1, 2)
    me = lax.axis_index("expert").astype(jnp.int32).reshape(1)

    other_rows, other_chosen = moved(rows, 0, 1), moved(chosen, 0, 1)
    held_rows, held_chosen = load(rows, chosen)
    outgoing = pl.pallas_call(
        functools.partial(pack_kernel, width, groups, flips, size),
        in_specs=[SMEM] + [VMEM] * 4,
        out_specs=[VMEM] * len(flips),
        out_shape=[jax.ShapeDtypeStruct((2 * size, features), jnp.bfloat16)] * len(flips),
        compiler_params=PARAMS,
        cost_estimate=CHEAP,
        name="pack",
    )(me, held_chosen, other_chosen, held_rows, other_rows)
    arrived = [moved(block, 1, i) for block, i in zip(outgoing, flips)]

    held = load(gate_weight[0], up_weight[0], down_weight[0])
    first = len(teams[0])
    out = list(run_experts(arrived[:first], 2 * size, norm_gain, *held))
    out += run_experts(arrived[first:], 2 * size, norm_gain, *held, after=out[:1])
    spare = -(experts + 1) % 16
    extra = [router[0].T, norm_gain, jnp.zeros((spare, features), jnp.bfloat16)]
    out[first - 1] = jnp.concatenate([out[first - 1]] + extra, axis=0)
    returned = [moved(block, -1, i) for block, i in zip(out, flips)]
    there = returned[first - 1][2 * size :]

    weights = pl.pallas_call(
        functools.partial(weight_kernel, width, groups, teams, size),
        in_specs=[SMEM, VMEM, VMEM, VMEM],
        out_specs=[VMEM] * 4,
        out_shape=[
            jax.ShapeDtypeStruct((2 * len(team) * size, batches * count), jnp.bfloat16)
            for _ in range(2)
            for team in teams
        ],
        compiler_params=PARAMS,
        cost_estimate=CHEAP,
        name="weights",
    )(me, chosen, rows, there)
    mine = [block[:size] for block in returned]
    mine += [moved(stacked(team, size, size), 0, 1) for team in (returned[:first], returned[first:])]
    high = jnp.concatenate(weights[0:2], axis=0)
    low = jnp.concatenate(weights[2:4], axis=0)
    mine = mine[:first] + [mine[-2]] + mine[first:-2] + [mine[-1]]
    return combine(rows, high, low, mine, jnp.bfloat16).reshape(tokens.shape)


def solution(mesh):
    placed = (
        P("section", None, "expert", None),
        P("section", None, None, "expert", None),
        P("section", None),
        P("section", None, None),
        P("section", None, "expert"),
        P("section", None, "expert"),
        P("section", "expert", None),
    )
    return jax.shard_map(
        shards,
        mesh=mesh,
        in_specs=placed,
        out_specs=P("section", None, "expert", None),
        check_vma=False,
    )
```

```python
import functools

import jax
import jax.numpy as jnp
from jax import lax
from jax.experimental import pallas as pl
from jax.experimental.pallas import tpu as pltpu
from jax.sharding import PartitionSpec as P

CAP = 20
epsilon = 1e-06
HOME = ("section", "expert")


def moved(block, by, flip):
    sections, width = lax.axis_size("section"), lax.axis_size("expert")
    pairs = [
        (s * width + e, (s + by) % sections * width + (e ^ flip))
        for s in range(sections)
        for e in range(width)
    ]
    return lax.ppermute(block, HOME, pairs)


def ranks(me, chosen, width, groups):
    tokens = chosen.shape[1]
    owner = lax.broadcasted_iota(jnp.int32, (width, tokens), 0) ^ me
    expert = owner // groups if groups > 1 else owner
    first = chosen[0:1, :] == expert
    match = first | (chosen[1:2, :] == expert)
    before = lax.broadcasted_iota(jnp.int32, (tokens, tokens), 0) < lax.broadcasted_iota(
        jnp.int32, (tokens, tokens), 1
    )
    rank = jnp.dot(
        match.astype(jnp.bfloat16), before.astype(jnp.bfloat16), preferred_element_type=jnp.float32
    ).astype(jnp.int32)
    return first, jnp.where(match, rank, -1)


def side_by_side(chosen_ref):
    return jnp.concatenate([chosen_ref[b] for b in range(chosen_ref.shape[0])], axis=1)


def pack_kernel(width, groups, flows, me_ref, *refs):
    chosen_refs, rows_refs, out_refs = refs[0:2], refs[2:4], refs[4:]
    for part in range(2):
        _, rank = ranks(me_ref[0], side_by_side(chosen_refs[part]), width, groups)
        rank = rank.astype(jnp.float32)
        select = []
        for flip, start, size in flows:
            place = lax.broadcasted_iota(jnp.int32, (size, rank.shape[1]), 0) + start
            select.append(jnp.where(rank[flip : flip + 1] == place.astype(jnp.float32), 1.0, 0.0))
        select = jnp.concatenate(select, axis=0).astype(jnp.bfloat16)
        packed = jnp.dot(select, rows_refs[part][...], preferred_element_type=jnp.float32)
        at = 0
        for out_ref, (_, _, size) in zip(out_refs, flows):
            out_ref[part * size : (part + 1) * size] = packed[at : at + size].astype(jnp.bfloat16)
            at += size


def weight_kernel(
    width, groups, order, me_ref, chosen_ref, rows_ref, there_ref, high_ref, low_ref
):
    chosen = side_by_side(chosen_ref)
    first, rank = ranks(me_ref[0], chosen, width, groups)
    experts = width // groups
    normed = normalised(rows_ref[...], there_ref[experts : experts + 1])
    logits = lax.dot_general(
        there_ref[0:experts], normed, (((1,), (1,)), ((), ())), preferred_element_type=jnp.float32
    )
    names = lax.broadcasted_iota(jnp.int32, logits.shape, 0)
    one = jnp.sum(jnp.where(names == chosen[0:1, :], logits, 0.0), axis=0, keepdims=True)
    two = jnp.sum(jnp.where(names == chosen[1:2, :], logits, 0.0), axis=0, keepdims=True)
    top = jnp.maximum(one, two)
    one, two = jnp.exp(one - top), jnp.exp(two - top)
    total = one + two
    weight = jnp.where(first, one / total, two / total)
    at = 0
    for flip, start, size in order:
        place = lax.broadcasted_iota(jnp.int32, (size, rank.shape[1]), 0) + start
        wide = jnp.where(rank[flip : flip + 1] == place, weight[flip : flip + 1], 0.0)
        high = wide.astype(jnp.bfloat16)
        high_ref[at : at + size] = high
        low_ref[at : at + size] = (wide - high.astype(jnp.float32)).astype(jnp.bfloat16)
        at += size


def normalised(rows, gain):
    wide = rows.astype(jnp.float32)
    scale = lax.rsqrt(jnp.mean(wide * wide, axis=-1, keepdims=True) + epsilon)
    return (wide * scale * gain.astype(jnp.float32)).astype(jnp.bfloat16)


def load_kernel(count, *refs):
    sources, held, sems = refs[:count], refs[-1 - count : -1], refs[-1]
    copies = [
        pltpu.make_async_copy(source, place, sems.at[k])
        for k, (source, place) in enumerate(zip(sources, held))
    ]
    for copy in copies:
        copy.start()
    for copy in copies:
        copy.wait()


def expert_kernel(sizes, ride, *refs):
    count = len(sizes)
    blocks, (gain_ref, router_ref), (gate_ref, up_ref, down_ref) = (
        refs[:count],
        refs[count : count + 2],
        refs[count + 2 : count + 5],
    )
    outs, (normed_ref, hidden_ref) = refs[-2 - count : -2], refs[-2:]
    gain = gain_ref[...]
    units, features = down_ref.shape
    if ride is not None:
        experts, size = router_ref.shape[0], sizes[ride]
        outs[ride][size:] = jnp.zeros((outs[ride].shape[0] - size, features), jnp.bfloat16)
        outs[ride][size : size + experts] = router_ref[...]
        outs[ride][size + experts : size + experts + 1] = gain
    starts = [sum(sizes[:j]) for j in range(count)]
    for j in range(count):
        normed_ref[starts[j] : starts[j] + sizes[j]] = normalised(blocks[j][0 : sizes[j]], gain)
    normed = normed_ref[...]
    step = min(256, units)
    for at in range(0, units, step):
        span = slice(at, at + step)
        gate = jnp.dot(normed, gate_ref[:, span], preferred_element_type=jnp.float32)
        up = jnp.dot(normed, up_ref[:, span], preferred_element_type=jnp.float32)
        hidden_ref[:, span] = (gate / (1.0 + jnp.exp(-gate)) * up).astype(jnp.bfloat16)
    hidden = hidden_ref[...]
    step = min(512, features)
    for at in range(0, features, step):
        span = slice(at, at + step)
        part = jnp.dot(hidden, down_ref[:, span], preferred_element_type=jnp.float32)
        part = part.astype(jnp.bfloat16)
        for j in range(count):
            outs[j][0 : sizes[j], span] = part[starts[j] : starts[j] + sizes[j]]


def tiles(length, step):
    return [slice(at, at + step) for at in range(0, length, step)]


def combine_kernel(base_ref, high_ref, low_ref, *refs):
    blocks, out_ref = refs[:-1], refs[-1]
    high, low = high_ref[...], low_ref[...]
    step = min(512, base_ref.shape[1])
    for at in range(0, base_ref.shape[1], step):
        span = slice(at, at + step)
        values = jnp.concatenate([ref[:, span] for ref in blocks], axis=0)
        total = base_ref[:, span].astype(jnp.float32)
        total += jnp.dot(high, values, preferred_element_type=jnp.float32)
        total += jnp.dot(low, values, preferred_element_type=jnp.float32)
        out_ref[:, span] = total.astype(out_ref.dtype)


def final_kernel(base_ref, high_ref, low_ref, values_ref, out_ref, done_ref, sems):
    high, low = high_ref[...], low_ref[...]
    copies = []
    for at, span in enumerate(tiles(base_ref.shape[1], min(512, base_ref.shape[1]))):
        values = values_ref[:, span]
        total = base_ref[:, span]
        total += jnp.dot(high, values, preferred_element_type=jnp.float32)
        total += jnp.dot(low, values, preferred_element_type=jnp.float32)
        done_ref[:, span] = total.astype(done_ref.dtype)
        copies.append(pltpu.make_async_copy(done_ref.at[:, span], out_ref.at[:, span], sems.at[at]))
        copies[-1].start()
    for copy in copies:
        copy.wait()


def stack_kernel(sizes, *refs):
    out_ref, at = refs[-1], 0
    for ref, size in zip(refs, sizes):
        out_ref[at : at + size] = ref[size : 2 * size]
        at += size


SMEM = pl.BlockSpec(memory_space=pltpu.SMEM)
VMEM = pl.BlockSpec(memory_space=pltpu.VMEM)
HBM = pl.BlockSpec(memory_space=pltpu.HBM)
ANY = pl.BlockSpec(memory_space=pl.ANY)
CHEAP = pl.CostEstimate(flops=1, bytes_accessed=1, transcendentals=0)
PARAMS = pltpu.CompilerParams(vmem_limit_bytes=20 * 1024 * 1024)


def load(*arrays):
    return pl.pallas_call(
        functools.partial(load_kernel, len(arrays)),
        in_specs=[HBM] * len(arrays),
        out_specs=[VMEM] * len(arrays),
        out_shape=[pltpu.VMEM(array.shape, array.dtype) for array in arrays],
        scratch_shapes=[pltpu.SemaphoreType.DMA((len(arrays),))],
        compiler_params=pltpu.CompilerParams(vmem_limit_bytes=1024 * 1024),
        cost_estimate=CHEAP,
        name="load",
    )(*[pltpu.with_memory_space_constraint(array, pltpu.HBM) for array in arrays])


def stacked(blocks, sizes):
    return pl.pallas_call(
        functools.partial(stack_kernel, sizes),
        in_specs=[VMEM] * len(blocks),
        out_specs=VMEM,
        out_shape=jax.ShapeDtypeStruct((sum(sizes), blocks[0].shape[1]), blocks[0].dtype),
        compiler_params=PARAMS,
        cost_estimate=CHEAP,
        name="stack",
    )(*blocks)


def finish(base, high, low, values):
    rows, features = base.shape
    return pl.pallas_call(
        final_kernel,
        in_specs=[VMEM] * 4,
        out_specs=HBM,
        out_shape=jax.ShapeDtypeStruct((rows, features), jnp.bfloat16),
        scratch_shapes=[
            pltpu.VMEM((rows, features), jnp.bfloat16),
            pltpu.SemaphoreType.DMA((len(tiles(features, min(512, features))),)),
        ],
        compiler_params=PARAMS,
        cost_estimate=CHEAP,
        name="finish",
    )(base, high.T, low.T, values)


def combine(base, high, low, blocks):
    return pl.pallas_call(
        combine_kernel,
        in_specs=[VMEM] * (3 + len(blocks)),
        out_specs=VMEM,
        out_shape=jax.ShapeDtypeStruct(base.shape, jnp.float32),
        compiler_params=PARAMS,
        cost_estimate=CHEAP,
        name="combine",
    )(base, high.T, low.T, *blocks)


def run_experts(blocks, sizes, ride, gain, router, held, after=()):
    count, features = len(blocks), gain.shape[1]
    rows, units = sum(sizes), held[0].shape[1]
    spare = -(-(router.shape[0] + 1) // 16) * 16
    return pl.pallas_call(
        functools.partial(expert_kernel, tuple(sizes), ride),
        in_specs=[VMEM] * (count + 5) + [ANY] * len(after),
        out_specs=[VMEM] * count,
        out_shape=[
            jax.ShapeDtypeStruct((size + (spare if j == ride else 0), features), jnp.bfloat16)
            for j, size in enumerate(sizes)
        ],
        scratch_shapes=[
            pltpu.VMEM((rows, features), jnp.bfloat16),
            pltpu.VMEM((rows, units), jnp.bfloat16),
        ],
        compiler_params=PARAMS,
        cost_estimate=CHEAP,
        name="experts",
    )(*blocks, gain, router, *held, *after)


FLOWS = ((3, 0, 16), (2, 0, 16), (1, 0, None), (0, 0, None), (3, 16, None), (2, 16, None))
TEAMS = ((0, 1, 3), (2,), (4, 5))
BACK = (0, 1, 4, 5, 2, 3)
RIDER = 3


def shards(tokens, routes, norm_gain, router, gate_weight, up_weight, down_weight):
    batches, count, features = tokens.shape[1:]
    experts = router.shape[2]
    width = lax.axis_size("expert")
    groups, size = width // experts, batches * CAP
    quarter = width // 4
    flows, members = [], []
    for band, start, stop in FLOWS:
        members.append([])
        for flip in range((band + 1) * quarter - 2, band * quarter - 1, -2):
            members[-1].append(len(flows))
            flows.append((flip, start, (size if stop is None else stop) - start))
    pick = lambda bands: [f for band in bands for f in members[band]]
    sizes = [2 * flow[2] for flow in flows]
    rows = tokens.reshape(batches * count, features)
    chosen = jnp.swapaxes(routes[0, 0], 1, 2)
    me = lax.axis_index("expert").astype(jnp.int32).reshape(1)

    other_rows, other_chosen = moved(rows, 0, 1), moved(chosen, 0, 1)
    held_rows, held_chosen = load(rows, chosen)
    outgoing = pl.pallas_call(
        functools.partial(pack_kernel, width, groups, flows),
        in_specs=[SMEM] + [VMEM] * 4,
        out_specs=[VMEM] * len(flows),
        out_shape=[jax.ShapeDtypeStruct((rows_of, features), jnp.bfloat16) for rows_of in sizes],
        compiler_params=PARAMS,
        cost_estimate=CHEAP,
        name="pack",
    )(me, held_chosen, other_chosen, held_rows, other_rows)
    arrived = [moved(block, 1, flow[0]) for block, flow in zip(outgoing, flows)]

    held = load(gate_weight[0], up_weight[0], down_weight[0])
    out, after = [None] * len(flows), []
    rider = pick([RIDER])[0]
    for team in TEAMS:
        mine = pick(team)
        results = run_experts(
            [arrived[f] for f in mine],
            [sizes[f] for f in mine],
            mine.index(rider) if rider in mine else None,
            norm_gain,
            router[0].T,
            held,
            after,
        )
        for f, result in zip(mine, results):
            out[f] = result
        after = [results[0]]
    returned = [None] * len(flows)
    for f in pick(BACK):
        returned[f] = moved(out[f], -1, flows[f][0])

    order = list(flows) + [(flip + 1, start, count) for flip, start, count in flows]
    high, low = pl.pallas_call(
        functools.partial(weight_kernel, width, groups, order),
        in_specs=[SMEM, VMEM, VMEM, VMEM],
        out_specs=[VMEM] * 2,
        out_shape=[jax.ShapeDtypeStruct((width * size, batches * count), jnp.bfloat16)] * 2,
        compiler_params=PARAMS,
        cost_estimate=CHEAP,
        name="weights",
    )(me, held_chosen, held_rows, returned[rider][sizes[rider] :])
    passed = moved(stacked(returned, [flow[2] for flow in flows]), 0, 1)
    own = [block[: flow[2]] for block, flow in zip(returned, flows)]
    half = width * size // 2
    total = combine(held_rows, high[:half], low[:half], own)
    return finish(total, high[half:], low[half:], passed).reshape(tokens.shape)


def solution(mesh):
    placed = (
        P("section", None, "expert", None),
        P("section", None, None, "expert", None),
        P("section", None),
        P("section", None, None),
        P("section", None, "expert"),
        P("section", None, "expert"),
        P("section", "expert", None),
    )
    return jax.shard_map(
        shards,
        mesh=mesh,
        in_specs=placed,
        out_specs=P("section", None, "expert", None),
        check_vma=False,
    )
```

```python
import functools

import jax
import jax.numpy as jnp
from jax import lax
from jax.experimental import pallas as pl
from jax.experimental.pallas import tpu as pltpu
from jax.sharding import PartitionSpec as P

CAP = 20
epsilon = 1e-06
HOME = ("section", "expert")


def moved(block, by, flip):
    sections, width = lax.axis_size("section"), lax.axis_size("expert")
    pairs = [
        (s * width + e, (s + by) % sections * width + (e ^ flip))
        for s in range(sections)
        for e in range(width)
    ]
    return lax.ppermute(block, HOME, pairs)


def ranks(me, chosen, width, groups):
    tokens = chosen.shape[1]
    owner = lax.broadcasted_iota(jnp.int32, (width, tokens), 0) ^ me
    expert = owner // groups if groups > 1 else owner
    first = chosen[0:1, :] == expert
    match = first | (chosen[1:2, :] == expert)
    before = lax.broadcasted_iota(jnp.int32, (tokens, tokens), 0) < lax.broadcasted_iota(
        jnp.int32, (tokens, tokens), 1
    )
    rank = jnp.dot(
        match.astype(jnp.bfloat16), before.astype(jnp.bfloat16), preferred_element_type=jnp.float32
    ).astype(jnp.int32)
    return first, jnp.where(match, rank, -1)


def side_by_side(chosen_ref):
    return jnp.concatenate([chosen_ref[b] for b in range(chosen_ref.shape[0])], axis=1)


def pack_kernel(width, groups, flows, me_ref, *refs):
    chosen_refs, rows_refs, out_refs = refs[0:2], refs[2:4], refs[4:]
    for part in range(2):
        _, rank = ranks(me_ref[0], side_by_side(chosen_refs[part]), width, groups)
        rank = rank.astype(jnp.float32)
        select = []
        for flip, start, size in flows:
            place = lax.broadcasted_iota(jnp.int32, (size, rank.shape[1]), 0) + start
            select.append(jnp.where(rank[flip : flip + 1] == place.astype(jnp.float32), 1.0, 0.0))
        select = jnp.concatenate(select, axis=0).astype(jnp.bfloat16)
        packed = jnp.dot(select, rows_refs[part][...], preferred_element_type=jnp.float32)
        at = 0
        for out_ref, (_, _, size) in zip(out_refs, flows):
            out_ref[part * size : (part + 1) * size] = packed[at : at + size].astype(jnp.bfloat16)
            at += size


def weight_kernel(
    width, groups, order, me_ref, chosen_ref, rows_ref, there_ref, high_ref, low_ref
):
    chosen = side_by_side(chosen_ref)
    first, rank = ranks(me_ref[0], chosen, width, groups)
    experts = width // groups
    normed = normalised(rows_ref[...], there_ref[experts : experts + 1])
    logits = lax.dot_general(
        there_ref[0:experts], normed, (((1,), (1,)), ((), ())), preferred_element_type=jnp.float32
    )
    names = lax.broadcasted_iota(jnp.int32, logits.shape, 0)
    one = jnp.sum(jnp.where(names == chosen[0:1, :], logits, 0.0), axis=0, keepdims=True)
    two = jnp.sum(jnp.where(names == chosen[1:2, :], logits, 0.0), axis=0, keepdims=True)
    top = jnp.maximum(one, two)
    one, two = jnp.exp(one - top), jnp.exp(two - top)
    total = one + two
    weight = jnp.where(first, one / total, two / total)
    at = 0
    for flip, start, size in order:
        place = lax.broadcasted_iota(jnp.int32, (size, rank.shape[1]), 0) + start
        wide = jnp.where(rank[flip : flip + 1] == place, weight[flip : flip + 1], 0.0)
        high = wide.astype(jnp.bfloat16)
        high_ref[at : at + size] = high
        low_ref[at : at + size] = (wide - high.astype(jnp.float32)).astype(jnp.bfloat16)
        at += size


def normalised(rows, gain):
    wide = rows.astype(jnp.float32)
    scale = lax.rsqrt(jnp.mean(wide * wide, axis=-1, keepdims=True) + epsilon)
    return (wide * scale * gain.astype(jnp.float32)).astype(jnp.bfloat16)


def load_kernel(count, *refs):
    sources, held, sems = refs[:count], refs[-1 - count : -1], refs[-1]
    copies = [
        pltpu.make_async_copy(source, place, sems.at[k])
        for k, (source, place) in enumerate(zip(sources, held))
    ]
    for copy in copies:
        copy.start()
    for copy in copies:
        copy.wait()


def expert_kernel(sizes, ride, *refs):
    count = len(sizes)
    blocks, (gain_ref, router_ref), (gate_ref, up_ref, down_ref) = (
        refs[:count],
        refs[count : count + 2],
        refs[count + 2 : count + 5],
    )
    outs, (normed_ref, hidden_ref) = refs[-2 - count : -2], refs[-2:]
    gain = gain_ref[...]
    units, features = down_ref.shape
    if ride is not None:
        experts, size = router_ref.shape[0], sizes[ride]
        outs[ride][size:] = jnp.zeros((outs[ride].shape[0] - size, features), jnp.bfloat16)
        outs[ride][size : size + experts] = router_ref[...]
        outs[ride][size + experts : size + experts + 1] = gain
    starts = [sum(sizes[:j]) for j in range(count)]
    for j in range(count):
        normed_ref[starts[j] : starts[j] + sizes[j]] = normalised(blocks[j][0 : sizes[j]], gain)
    normed = normed_ref[...]
    step = min(256, units)
    for at in range(0, units, step):
        span = slice(at, at + step)
        gate = jnp.dot(normed, gate_ref[:, span], preferred_element_type=jnp.float32)
        up = jnp.dot(normed, up_ref[:, span], preferred_element_type=jnp.float32)
        hidden_ref[:, span] = (gate / (1.0 + jnp.exp(-gate)) * up).astype(jnp.bfloat16)
    hidden = hidden_ref[...]
    step = min(512, features)
    for at in range(0, features, step):
        span = slice(at, at + step)
        part = jnp.dot(hidden, down_ref[:, span], preferred_element_type=jnp.float32)
        part = part.astype(jnp.bfloat16)
        for j in range(count):
            outs[j][0 : sizes[j], span] = part[starts[j] : starts[j] + sizes[j]]


def tiles(length, step):
    return [slice(at, at + step) for at in range(0, length, step)]


def combine_kernel(base_ref, high_ref, low_ref, *refs):
    blocks, out_ref = refs[:-1], refs[-1]
    high, low = high_ref[...], low_ref[...]
    step = min(512, base_ref.shape[1])
    for at in range(0, base_ref.shape[1], step):
        span = slice(at, at + step)
        values = jnp.concatenate([ref[:, span] for ref in blocks], axis=0)
        total = base_ref[:, span].astype(jnp.float32)
        total += jnp.dot(high, values, preferred_element_type=jnp.float32)
        total += jnp.dot(low, values, preferred_element_type=jnp.float32)
        out_ref[:, span] = total.astype(out_ref.dtype)


def final_kernel(base_ref, high_ref, low_ref, *refs):
    blocks, (out_ref, done_ref, sems) = refs[:-3], refs[-3:]
    high, low = high_ref[...], low_ref[...]
    copies = []
    for at, span in enumerate(tiles(base_ref.shape[1], min(512, base_ref.shape[1]))):
        values = jnp.concatenate([ref[:, span] for ref in blocks], axis=0)
        total = base_ref[:, span]
        total += jnp.dot(high, values, preferred_element_type=jnp.float32)
        total += jnp.dot(low, values, preferred_element_type=jnp.float32)
        done_ref[:, span] = total.astype(done_ref.dtype)
        copies.append(pltpu.make_async_copy(done_ref.at[:, span], out_ref.at[:, span], sems.at[at]))
        copies[-1].start()
    for copy in copies:
        copy.wait()


def stack_kernel(sizes, *refs):
    out_ref, at = refs[-1], 0
    for ref, size in zip(refs, sizes):
        out_ref[at : at + size] = ref[size : 2 * size]
        at += size


SMEM = pl.BlockSpec(memory_space=pltpu.SMEM)
VMEM = pl.BlockSpec(memory_space=pltpu.VMEM)
HBM = pl.BlockSpec(memory_space=pltpu.HBM)
ANY = pl.BlockSpec(memory_space=pl.ANY)
CHEAP = pl.CostEstimate(flops=1, bytes_accessed=1, transcendentals=0)
PARAMS = pltpu.CompilerParams(vmem_limit_bytes=20 * 1024 * 1024)


def load(*arrays):
    return pl.pallas_call(
        functools.partial(load_kernel, len(arrays)),
        in_specs=[HBM] * len(arrays),
        out_specs=[VMEM] * len(arrays),
        out_shape=[pltpu.VMEM(array.shape, array.dtype) for array in arrays],
        scratch_shapes=[pltpu.SemaphoreType.DMA((len(arrays),))],
        compiler_params=pltpu.CompilerParams(vmem_limit_bytes=1024 * 1024),
        cost_estimate=CHEAP,
        name="load",
    )(*[pltpu.with_memory_space_constraint(array, pltpu.HBM) for array in arrays])


def stacked(blocks, sizes):
    return pl.pallas_call(
        functools.partial(stack_kernel, sizes),
        in_specs=[VMEM] * len(blocks),
        out_specs=VMEM,
        out_shape=jax.ShapeDtypeStruct((sum(sizes), blocks[0].shape[1]), blocks[0].dtype),
        compiler_params=PARAMS,
        cost_estimate=CHEAP,
        name="stack",
    )(*blocks)


def finish(base, high, low, blocks):
    rows, features = base.shape
    return pl.pallas_call(
        final_kernel,
        in_specs=[VMEM] * (3 + len(blocks)),
        out_specs=HBM,
        out_shape=jax.ShapeDtypeStruct((rows, features), jnp.bfloat16),
        scratch_shapes=[
            pltpu.VMEM((rows, features), jnp.bfloat16),
            pltpu.SemaphoreType.DMA((len(tiles(features, min(512, features))),)),
        ],
        compiler_params=PARAMS,
        cost_estimate=CHEAP,
        name="finish",
    )(base, high.T, low.T, *blocks)


def combine(base, high, low, blocks):
    return pl.pallas_call(
        combine_kernel,
        in_specs=[VMEM] * (3 + len(blocks)),
        out_specs=VMEM,
        out_shape=jax.ShapeDtypeStruct(base.shape, jnp.float32),
        compiler_params=PARAMS,
        cost_estimate=CHEAP,
        name="combine",
    )(base, high.T, low.T, *blocks)


def run_experts(blocks, sizes, ride, gain, router, held, after=()):
    count, features = len(blocks), gain.shape[1]
    rows, units = sum(sizes), held[0].shape[1]
    spare = -(-(router.shape[0] + 1) // 16) * 16
    return pl.pallas_call(
        functools.partial(expert_kernel, tuple(sizes), ride),
        in_specs=[VMEM] * (count + 5) + [ANY] * len(after),
        out_specs=[VMEM] * count,
        out_shape=[
            jax.ShapeDtypeStruct((size + (spare if j == ride else 0), features), jnp.bfloat16)
            for j, size in enumerate(sizes)
        ],
        scratch_shapes=[
            pltpu.VMEM((rows, features), jnp.bfloat16),
            pltpu.VMEM((rows, units), jnp.bfloat16),
        ],
        compiler_params=PARAMS,
        cost_estimate=CHEAP,
        name="experts",
    )(*blocks, gain, router, *held, *after)


FLOWS = ((3, 0, 16), (2, 0, 16), (1, 0, None), (0, 0, None), (3, 16, None), (2, 16, None))
TEAMS = ((0, 3), (1, 2), (4, 5))
BACK = (0, 1, 4, 5, 2, 3)
RIDER = 3
SWAPS = ((0, 1, 4, 5, 3), (2,))


def shards(tokens, routes, norm_gain, router, gate_weight, up_weight, down_weight):
    batches, count, features = tokens.shape[1:]
    experts = router.shape[2]
    width = lax.axis_size("expert")
    groups, size = width // experts, batches * CAP
    quarter = width // 4
    flows, members = [], []
    for band, start, stop in FLOWS:
        members.append([])
        for flip in range((band + 1) * quarter - 2, band * quarter - 1, -2):
            members[-1].append(len(flows))
            flows.append((flip, start, (size if stop is None else stop) - start))
    pick = lambda bands: [f for band in bands for f in members[band]]
    sizes = [2 * flow[2] for flow in flows]
    rows = tokens.reshape(batches * count, features)
    chosen = jnp.swapaxes(routes[0, 0], 1, 2)
    me = lax.axis_index("expert").astype(jnp.int32).reshape(1)

    other_rows, other_chosen = moved(rows, 0, 1), moved(chosen, 0, 1)
    held_rows, held_chosen = load(rows, chosen)
    outgoing = pl.pallas_call(
        functools.partial(pack_kernel, width, groups, flows),
        in_specs=[SMEM] + [VMEM] * 4,
        out_specs=[VMEM] * len(flows),
        out_shape=[jax.ShapeDtypeStruct((rows_of, features), jnp.bfloat16) for rows_of in sizes],
        compiler_params=PARAMS,
        cost_estimate=CHEAP,
        name="pack",
    )(me, held_chosen, other_chosen, held_rows, other_rows)
    arrived = [moved(block, 1, flow[0]) for block, flow in zip(outgoing, flows)]

    held = load(gate_weight[0], up_weight[0], down_weight[0])
    out, after = [None] * len(flows), []
    rider = pick([RIDER])[0]
    for team in TEAMS:
        mine = pick(team)
        results = run_experts(
            [arrived[f] for f in mine],
            [sizes[f] for f in mine],
            mine.index(rider) if rider in mine else None,
            norm_gain,
            router[0].T,
            held,
            after,
        )
        for f, result in zip(mine, results):
            out[f] = result
        after = [results[0]]
    returned = [None] * len(flows)
    for f in pick(BACK):
        returned[f] = moved(out[f], -1, flows[f][0])

    early, late = pick(SWAPS[0]), pick(SWAPS[1])
    order = [flows[f] for f in early + late]
    order += [(flip + 1, start, taken) for flip, start, taken in order]
    high, low = pl.pallas_call(
        functools.partial(weight_kernel, width, groups, order),
        in_specs=[SMEM, VMEM, VMEM, VMEM],
        out_specs=[VMEM] * 2,
        out_shape=[jax.ShapeDtypeStruct((width * size, batches * count), jnp.bfloat16)] * 2,
        compiler_params=PARAMS,
        cost_estimate=CHEAP,
        name="weights",
    )(me, held_chosen, held_rows, returned[rider][sizes[rider] :])
    mine = [[returned[f][: flows[f][2]] for f in part] for part in (early, late)]
    passed = [
        moved(stacked([returned[f] for f in part], [flows[f][2] for f in part]), 0, 1)
        for part in (early, late)
    ]
    split = sum(block.shape[0] for block in mine[0])
    total = combine(held_rows, high[:split], low[:split], mine[0])
    return finish(total, high[split:], low[split:], mine[1] + passed).reshape(tokens.shape)


def solution(mesh):
    placed = (
        P("section", None, "expert", None),
        P("section", None, None, "expert", None),
        P("section", None),
        P("section", None, None),
        P("section", None, "expert"),
        P("section", None, "expert"),
        P("section", "expert", None),
    )
    return jax.shard_map(
        shards,
        mesh=mesh,
        in_specs=placed,
        out_specs=P("section", None, "expert", None),
        check_vma=False,
    )
```

```python
import functools

import jax
import jax.numpy as jnp
from jax import lax
from jax.experimental import pallas as pl
from jax.experimental.pallas import tpu as pltpu
from jax.sharding import PartitionSpec as P

CAP = 20
epsilon = 1e-06
HOME = ("section", "expert")


def moved(block, by, flip):
    sections, width = lax.axis_size("section"), lax.axis_size("expert")
    pairs = [
        (s * width + e, (s + by) % sections * width + (e ^ flip))
        for s in range(sections)
        for e in range(width)
    ]
    return lax.ppermute(block, HOME, pairs)


def ranks(me, chosen, width, groups):
    tokens = chosen.shape[1]
    owner = lax.broadcasted_iota(jnp.int32, (width, tokens), 0) ^ me
    expert = owner // groups if groups > 1 else owner
    first = chosen[0:1, :] == expert
    match = first | (chosen[1:2, :] == expert)
    before = lax.broadcasted_iota(jnp.int32, (tokens, tokens), 0) < lax.broadcasted_iota(
        jnp.int32, (tokens, tokens), 1
    )
    rank = jnp.dot(
        match.astype(jnp.bfloat16), before.astype(jnp.bfloat16), preferred_element_type=jnp.float32
    ).astype(jnp.int32)
    return first, jnp.where(match, rank, -1)


def side_by_side(chosen_ref):
    return jnp.concatenate([chosen_ref[b] for b in range(chosen_ref.shape[0])], axis=1)


def pack_kernel(width, groups, flows, me_ref, *refs):
    chosen_refs, rows_refs, out_refs = refs[0:2], refs[2:4], refs[4:]
    for part in range(2):
        _, rank = ranks(me_ref[0], side_by_side(chosen_refs[part]), width, groups)
        rank = rank.astype(jnp.float32)
        select = []
        for flip, start, size in flows:
            place = lax.broadcasted_iota(jnp.int32, (size, rank.shape[1]), 0) + start
            select.append(jnp.where(rank[flip : flip + 1] == place.astype(jnp.float32), 1.0, 0.0))
        select = jnp.concatenate(select, axis=0).astype(jnp.bfloat16)
        packed = jnp.dot(select, rows_refs[part][...], preferred_element_type=jnp.float32)
        at = 0
        for out_ref, (_, _, size) in zip(out_refs, flows):
            out_ref[part * size : (part + 1) * size] = packed[at : at + size].astype(jnp.bfloat16)
            at += size


def weight_kernel(
    width, groups, order, me_ref, chosen_ref, rows_ref, there_ref, high_ref, low_ref
):
    chosen = side_by_side(chosen_ref)
    first, rank = ranks(me_ref[0], chosen, width, groups)
    experts = width // groups
    normed = normalised(rows_ref[...], there_ref[experts : experts + 1])
    logits = lax.dot_general(
        there_ref[0:experts], normed, (((1,), (1,)), ((), ())), preferred_element_type=jnp.float32
    )
    names = lax.broadcasted_iota(jnp.int32, logits.shape, 0)
    one = jnp.sum(jnp.where(names == chosen[0:1, :], logits, 0.0), axis=0, keepdims=True)
    two = jnp.sum(jnp.where(names == chosen[1:2, :], logits, 0.0), axis=0, keepdims=True)
    top = jnp.maximum(one, two)
    one, two = jnp.exp(one - top), jnp.exp(two - top)
    total = one + two
    weight = jnp.where(first, one / total, two / total)
    at = 0
    for flip, start, size in order:
        place = lax.broadcasted_iota(jnp.int32, (size, rank.shape[1]), 0) + start
        wide = jnp.where(rank[flip : flip + 1] == place, weight[flip : flip + 1], 0.0)
        high = wide.astype(jnp.bfloat16)
        high_ref[at : at + size] = high
        low_ref[at : at + size] = (wide - high.astype(jnp.float32)).astype(jnp.bfloat16)
        at += size


def normalised(rows, gain):
    wide = rows.astype(jnp.float32)
    scale = lax.rsqrt(jnp.mean(wide * wide, axis=-1, keepdims=True) + epsilon)
    return (wide * scale * gain.astype(jnp.float32)).astype(jnp.bfloat16)


def load_kernel(count, *refs):
    sources, held, sems = refs[:count], refs[-1 - count : -1], refs[-1]
    copies = [
        pltpu.make_async_copy(source, place, sems.at[k])
        for k, (source, place) in enumerate(zip(sources, held))
    ]
    for copy in copies:
        copy.start()
    for copy in copies:
        copy.wait()


def expert_kernel(sizes, ride, *refs):
    count = len(sizes)
    blocks, (gain_ref, router_ref), (gate_ref, up_ref, down_ref) = (
        refs[:count],
        refs[count : count + 2],
        refs[count + 2 : count + 5],
    )
    outs, (normed_ref, hidden_ref) = refs[-2 - count : -2], refs[-2:]
    gain = gain_ref[...]
    units, features = down_ref.shape
    if ride is not None:
        experts, size = router_ref.shape[0], sizes[ride]
        outs[ride][size:] = jnp.zeros((outs[ride].shape[0] - size, features), jnp.bfloat16)
        outs[ride][size : size + experts] = router_ref[...]
        outs[ride][size + experts : size + experts + 1] = gain
    starts = [sum(sizes[:j]) for j in range(count)]
    for j in range(count):
        normed_ref[starts[j] : starts[j] + sizes[j]] = normalised(blocks[j][0 : sizes[j]], gain)
    normed = normed_ref[...]
    step = min(256, units)
    for at in range(0, units, step):
        span = slice(at, at + step)
        gate = jnp.dot(normed, gate_ref[:, span], preferred_element_type=jnp.float32)
        up = jnp.dot(normed, up_ref[:, span], preferred_element_type=jnp.float32)
        hidden_ref[:, span] = (gate / (1.0 + jnp.exp(-gate)) * up).astype(jnp.bfloat16)
    hidden = hidden_ref[...]
    step = min(512, features)
    for at in range(0, features, step):
        span = slice(at, at + step)
        part = jnp.dot(hidden, down_ref[:, span], preferred_element_type=jnp.float32)
        part = part.astype(jnp.bfloat16)
        for j in range(count):
            outs[j][0 : sizes[j], span] = part[starts[j] : starts[j] + sizes[j]]


def tiles(length, step):
    return [slice(at, at + step) for at in range(0, length, step)]


def combine_kernel(base_ref, high_ref, low_ref, *refs):
    blocks, out_ref = refs[:-1], refs[-1]
    high, low = high_ref[...], low_ref[...]
    step = min(512, base_ref.shape[1])
    for at in range(0, base_ref.shape[1], step):
        span = slice(at, at + step)
        values = jnp.concatenate([ref[:, span] for ref in blocks], axis=0)
        total = base_ref[:, span].astype(jnp.float32)
        total += jnp.dot(high, values, preferred_element_type=jnp.float32)
        total += jnp.dot(low, values, preferred_element_type=jnp.float32)
        out_ref[:, span] = total.astype(out_ref.dtype)


def final_kernel(base_ref, high_ref, low_ref, *refs):
    blocks, (out_ref, done_ref, sems) = refs[:-3], refs[-3:]
    high, low = high_ref[...], low_ref[...]
    copies = []
    for at, span in enumerate(tiles(base_ref.shape[1], min(1024, base_ref.shape[1]))):
        values = jnp.concatenate([ref[:, span] for ref in blocks], axis=0)
        total = base_ref[:, span]
        total += jnp.dot(high, values, preferred_element_type=jnp.float32)
        total += jnp.dot(low, values, preferred_element_type=jnp.float32)
        done_ref[:, span] = total.astype(done_ref.dtype)
        copies.append(pltpu.make_async_copy(done_ref.at[:, span], out_ref.at[:, span], sems.at[at]))
        copies[-1].start()
    for copy in copies:
        copy.wait()


def stack_kernel(sizes, *refs):
    out_ref, at = refs[-1], 0
    for ref, size in zip(refs, sizes):
        out_ref[at : at + size] = ref[size : 2 * size]
        at += size


SMEM = pl.BlockSpec(memory_space=pltpu.SMEM)
VMEM = pl.BlockSpec(memory_space=pltpu.VMEM)
HBM = pl.BlockSpec(memory_space=pltpu.HBM)
ANY = pl.BlockSpec(memory_space=pl.ANY)
CHEAP = pl.CostEstimate(flops=1, bytes_accessed=1, transcendentals=0)
PARAMS = pltpu.CompilerParams(vmem_limit_bytes=20 * 1024 * 1024)


def load(*arrays):
    return pl.pallas_call(
        functools.partial(load_kernel, len(arrays)),
        in_specs=[HBM] * len(arrays),
        out_specs=[VMEM] * len(arrays),
        out_shape=[pltpu.VMEM(array.shape, array.dtype) for array in arrays],
        scratch_shapes=[pltpu.SemaphoreType.DMA((len(arrays),))],
        compiler_params=pltpu.CompilerParams(vmem_limit_bytes=1024 * 1024),
        cost_estimate=CHEAP,
        name="load",
    )(*[pltpu.with_memory_space_constraint(array, pltpu.HBM) for array in arrays])


def stacked(blocks, sizes):
    return pl.pallas_call(
        functools.partial(stack_kernel, sizes),
        in_specs=[VMEM] * len(blocks),
        out_specs=VMEM,
        out_shape=jax.ShapeDtypeStruct((sum(sizes), blocks[0].shape[1]), blocks[0].dtype),
        compiler_params=PARAMS,
        cost_estimate=CHEAP,
        name="stack",
    )(*blocks)


def finish(base, high, low, blocks):
    rows, features = base.shape
    return pl.pallas_call(
        final_kernel,
        in_specs=[VMEM] * (3 + len(blocks)),
        out_specs=HBM,
        out_shape=jax.ShapeDtypeStruct((rows, features), jnp.bfloat16),
        scratch_shapes=[
            pltpu.VMEM((rows, features), jnp.bfloat16),
            pltpu.SemaphoreType.DMA((len(tiles(features, min(1024, features))),)),
        ],
        compiler_params=PARAMS,
        cost_estimate=CHEAP,
        name="finish",
    )(base, high.T, low.T, *blocks)


def combine(base, high, low, blocks):
    return pl.pallas_call(
        combine_kernel,
        in_specs=[VMEM] * (3 + len(blocks)),
        out_specs=VMEM,
        out_shape=jax.ShapeDtypeStruct(base.shape, jnp.float32),
        compiler_params=PARAMS,
        cost_estimate=CHEAP,
        name="combine",
    )(base, high.T, low.T, *blocks)


def run_experts(blocks, sizes, ride, gain, router, held, after=()):
    count, features = len(blocks), gain.shape[1]
    rows, units = sum(sizes), held[0].shape[1]
    spare = -(-(router.shape[0] + 1) // 16) * 16
    return pl.pallas_call(
        functools.partial(expert_kernel, tuple(sizes), ride),
        in_specs=[VMEM] * (count + 5) + [ANY] * len(after),
        out_specs=[VMEM] * count,
        out_shape=[
            jax.ShapeDtypeStruct((size + (spare if j == ride else 0), features), jnp.bfloat16)
            for j, size in enumerate(sizes)
        ],
        scratch_shapes=[
            pltpu.VMEM((rows, features), jnp.bfloat16),
            pltpu.VMEM((rows, units), jnp.bfloat16),
        ],
        compiler_params=PARAMS,
        cost_estimate=CHEAP,
        name="experts",
    )(*blocks, gain, router, *held, *after)


FLOWS = ((3, 0, 16), (2, 0, 16), (1, 0, None), (0, 0, None), (3, 16, None), (2, 16, None))
TEAMS = ((0, 3), (1, 2), (4, 5))
BACK = (0, 1, 4, 5, 2, 3)
RIDER = 3
PACKS = ((2, 3, 0), (1, 4, 5))
SWAPS = ((0, 1, 4, 5, 3), (2,))


def shards(tokens, routes, norm_gain, router, gate_weight, up_weight, down_weight):
    batches, count, features = tokens.shape[1:]
    experts = router.shape[2]
    width = lax.axis_size("expert")
    groups, size = width // experts, batches * CAP
    quarter = width // 4
    flows, members = [], []
    for band, start, stop in FLOWS:
        members.append([])
        for flip in range((band + 1) * quarter - 2, band * quarter - 1, -2):
            members[-1].append(len(flows))
            flows.append((flip, start, (size if stop is None else stop) - start))
    pick = lambda bands: [f for band in bands for f in members[band]]
    sizes = [2 * flow[2] for flow in flows]
    rows = tokens.reshape(batches * count, features)
    chosen = jnp.swapaxes(routes[0, 0], 1, 2)
    me = lax.axis_index("expert").astype(jnp.int32).reshape(1)

    other_rows, other_chosen = moved(rows, 0, 1), moved(chosen, 0, 1)
    held_rows, held_chosen = load(rows, chosen)
    def pack(part):
        return pl.pallas_call(
            functools.partial(pack_kernel, width, groups, [flows[f] for f in part]),
            in_specs=[SMEM] + [VMEM] * 4,
            out_specs=[VMEM] * len(part),
            out_shape=[jax.ShapeDtypeStruct((sizes[f], features), jnp.bfloat16) for f in part],
            compiler_params=PARAMS,
            cost_estimate=CHEAP,
            name="pack",
        )(me, held_chosen, other_chosen, held_rows, other_rows)

    outgoing = [None] * len(flows)
    for part in (pick(PACKS[0]), pick(PACKS[1])):
        for f, block in zip(part, pack(part)):
            outgoing[f] = block
    arrived = [moved(block, 1, flow[0]) for block, flow in zip(outgoing, flows)]

    held = load(gate_weight[0], up_weight[0], down_weight[0])
    out, after = [None] * len(flows), []
    rider = pick([RIDER])[0]
    for team in TEAMS:
        mine = pick(team)
        results = run_experts(
            [arrived[f] for f in mine],
            [sizes[f] for f in mine],
            mine.index(rider) if rider in mine else None,
            norm_gain,
            router[0].T,
            held,
            after,
        )
        for f, result in zip(mine, results):
            out[f] = result
        after = [results[0]]
    returned = [None] * len(flows)
    for f in pick(BACK):
        returned[f] = moved(out[f], -1, flows[f][0])

    early, late = pick(SWAPS[0]), pick(SWAPS[1])
    order = [flows[f] for f in early + late]
    order += [(flip + 1, start, taken) for flip, start, taken in order]
    high, low = pl.pallas_call(
        functools.partial(weight_kernel, width, groups, order),
        in_specs=[SMEM, VMEM, VMEM, VMEM],
        out_specs=[VMEM] * 2,
        out_shape=[jax.ShapeDtypeStruct((width * size, batches * count), jnp.bfloat16)] * 2,
        compiler_params=PARAMS,
        cost_estimate=CHEAP,
        name="weights",
    )(me, held_chosen, held_rows, returned[rider][sizes[rider] :])
    mine = [[returned[f][: flows[f][2]] for f in part] for part in (early, late)]
    passed = [
        moved(stacked([returned[f] for f in part], [flows[f][2] for f in part]), 0, 1)
        for part in (early, late)
    ]
    split = sum(block.shape[0] for block in mine[0])
    total = combine(held_rows, high[:split], low[:split], mine[0])
    return finish(total, high[split:], low[split:], mine[1] + passed).reshape(tokens.shape)


def solution(mesh):
    placed = (
        P("section", None, "expert", None),
        P("section", None, None, "expert", None),
        P("section", None),
        P("section", None, None),
        P("section", None, "expert"),
        P("section", None, "expert"),
        P("section", "expert", None),
    )
    return jax.shard_map(
        shards,
        mesh=mesh,
        in_specs=placed,
        out_specs=P("section", None, "expert", None),
        check_vma=False,
    )
```
